256 devices in a mesh: win: 16 (over x_hi, z), atom: 16 (over x_lo, y, core).
Axes of the slice: x: 4 (x_hi: 2, x_lo: 2; x = x_hi * 2 + x_lo), y: 4, z: 8, core: 2. Of those that a mesh axis runs over, the one named last changes fastest.
Arguments:
- retarded: bfloat16 [512, 32, 2, 128, 128], P(('win', 'atom')), may hold values from -0.375 to 0.375
- sigma_in: bfloat16 [512, 32, 2, 128, 128], P(('win', 'atom')), may hold values from -6 to 6
- bit_shifts: int32 [3], replicated, may hold values from 0 to 3, as said below
- occupation: float32 [3], replicated, may hold values from 0.3 to 3
- neighbors: int32 [32, 3], replicated, may hold values from 0 to 31, as said below
- coupling: bfloat16 [3, 128, 128], replicated, may hold values from -0.375 to 0.375
Outputs:
- self_energy: bfloat16 [512, 32, 2, 128, 128], P('win', 'atom')
The draws below stay inside these ranges and needn't reach their ends.
Inputs may be any that keep to these rules, and one draw needn't show every extreme that they name: `bit_shifts`: three different values; among them are 0 and 3, in an order drawn afresh. `neighbors`: column 0 of row b is b itself; the other columns of row b lie within b - 1 to b + 1.
All inputs are finite; a program needn't handle non-finite values.
Results may differ from the reference program's by a relative error of at most 0.007.
Values may be sent and summed in bfloat16 or wider, within the bound.
A program may use at most 128 MiB of HBM per device.

```python
import math
import jax
import jax.numpy as jnp
from jax import lax

NORB = 128
MODES = 3
DIRS = 3
EW = 32
NE = 512
NB = 32
WBITS = 4
N_WIN = 16


def draw_bit_shifts(key, part):
    middle = jax.random.randint(key, (), 1, WBITS - 1).astype(jnp.int32)
    values = jnp.stack([jnp.int32(0), middle, jnp.int32(WBITS - 1)])
    order = jax.random.permutation(jax.random.fold_in(key, 7), 3)
    return values[order].astype(jnp.int32)


def draw_neighbors(key, part):
    offsets = jax.random.randint(key, (NB, DIRS - 1), -1, 2).astype(jnp.int32)
    blocks = jnp.arange(NB, dtype=jnp.int32)[:, None]
    others = jnp.clip(blocks + offsets, 0, NB - 1)
    return jnp.concatenate([blocks, others], axis=1).astype(jnp.int32)


def level_of(key, extent, cuts, smallest, largest):
    gain, own = 1.0, jax.random.fold_in(key, 6)
    for axis_at, blocks in cuts:
        heights = jnp.exp(jax.random.uniform(jax.random.fold_in(own, axis_at), (blocks,), jnp.float32, smallest / len(cuts), largest / len(cuts)))
        gain = gain * jnp.repeat(heights, extent[axis_at] // blocks).reshape([-1 if axis == axis_at else 1 for axis in range(len(extent))])
    return gain


def bell_draw(rng, dims, scale, most, cuts=(), kind=jnp.bfloat16):
    entries = jax.random.normal(rng, dims, jnp.float32) * scale
    if len(cuts) > 0:
        entries = level_of(rng, dims, cuts, -0.22, 0.18) * entries
    return jnp.clip(entries, min=-most, max=most).astype(kind)


def setup_inputs(seed: int = 0) -> dict:
    key_of = jax.random.split(jax.random.key(seed), 7)
    retarded = bell_draw(key_of[0], (NE, NB, 2, NORB, NORB), (2 * NORB) ** -0.5, 0.375, ((0, 256),))
    sigma_in = bell_draw(key_of[1], (NE, NB, 2, NORB, NORB), 1.0, 6.0, ((0, 256),))
    bit_shifts = draw_bit_shifts(jax.random.fold_in(key_of[6], 71), 0)
    occupation = jnp.clip(jnp.exp(jax.random.uniform(key_of[3], (MODES,), jnp.float32, math.log(0.3), math.log(3.0))), 0.3, 3.0)
    neighbors = draw_neighbors(jax.random.fold_in(key_of[6], 71), 0)
    coupling = bell_draw(key_of[5], (DIRS, NORB, NORB), (2 * NORB) ** -0.5, 0.375)
    return dict(retarded=retarded, sigma_in=sigma_in, bit_shifts=bit_shifts, occupation=occupation, neighbors=neighbors, coupling=coupling)


def complex_product(left, right, form):
    left = left.astype(jnp.float32)
    right = right.astype(jnp.float32)
    real_part = jnp.einsum(form, left[:, 0], right[:, 0]) - jnp.einsum(form, left[:, 1], right[:, 1])
    imag_part = jnp.einsum(form, left[:, 0], right[:, 1]) + jnp.einsum(form, left[:, 1], right[:, 0])
    return jnp.stack([real_part, imag_part], axis=1).astype(jnp.bfloat16)


def reference(retarded, sigma_in, bit_shifts, occupation, neighbors, coupling):
    def lesser_one(pair):
        green_one, sigma_one = pair
        product = complex_product(green_one, sigma_one, 'bij,bjk->bik')
        product = lax.optimization_barrier(product)
        return complex_product(product, green_one, 'bij,bkj->bik')

    lesser = lax.map(lesser_one, (retarded, sigma_in))
    windows = lesser.reshape(N_WIN, EW, NB, 2, NORB, NORB)
    coupling_f = coupling.astype(jnp.float32)

    def window_self(window):
        summed = jnp.zeros((EW, NB, 2, NORB, NORB), jnp.float32)
        for mode in range(MODES):
            partner = jnp.bitwise_xor(window, jnp.left_shift(jnp.int32(1), bit_shifts[mode]))
            summed = summed + occupation[mode] * windows[partner].astype(jnp.float32)
        partners = lax.optimization_barrier(summed.astype(jnp.bfloat16)).astype(jnp.float32)
        result = jnp.zeros((EW, NB, 2, NORB, NORB), jnp.float32)
        for direction in range(DIRS):
            picked = jnp.take(partners, neighbors[:, direction], axis=1)
            bent = jnp.einsum('ij,erxjk->erxik', coupling_f[direction], picked).astype(jnp.bfloat16)
            bent = lax.optimization_barrier(bent).astype(jnp.float32)
            result = result + jnp.einsum('erxij,kj->erxik', bent, coupling_f[direction])
        return result.astype(jnp.bfloat16)

    output = lax.map(window_self, jnp.arange(N_WIN, dtype=jnp.int32))
    return output.reshape(NE, NB, 2, NORB, NORB)
```

```python
import functools

import jax
import jax.numpy as jnp
from jax import lax
from jax.experimental import pallas as pl
from jax.experimental.pallas import tpu as pltpu
from jax.sharding import PartitionSpec as P

MESH = pl.DeviceIdType.MESH
F32 = jnp.float32
BF16 = jnp.bfloat16


def dot(left, right, contract):
    return lax.dot_general(left, right, ((contract[0:1], contract[1:2]), ((), ())), preferred_element_type=F32)


def fold(quad, norb):
    real = quad[:norb, :norb] - quad[norb:, norb:]
    imag = quad[:norb, norb:] + quad[norb:, :norb]
    return jnp.concatenate([real, imag], axis=0).astype(BF16)


def flip(win, bit):
    mask = 2**bit
    return win + mask * (1 - 2 * ((win // mask) % 2))


def kernel(
    bits,
    n_atom,
    shifts_ref,
    occ_ref,
    near_ref,
    green_hbm,
    sigma_hbm,
    coupling_ref,
    out_ref,
    green,
    sigma,
    lesser,
    part,
    got,
    total,
    in_sem,
    send_sem,
    recv_sem,
    give_sem,
    take_sem,
    own_sem,
):
    steps = n_atom
    own_e = green.shape[0]
    own_b = lesser.shape[1] // n_atom
    norb = green.shape[-1]
    win = lax.axis_index("win")
    atom = lax.axis_index("atom")
    partners = [flip(win, bit) for bit in bits]

    def owner(step):
        return lax.rem(atom + 1 + step, n_atom)

    def load(kind, j):
        source, target = ((green_hbm, green), (sigma_hbm, sigma))[kind]
        rows = pl.ds(j * own_b, own_b)
        return pltpu.make_async_copy(source.at[:, rows], target.at[:, rows], in_sem.at[kind, j])

    @pl.loop(0, n_atom)
    def _(i):
        j = lax.rem(atom + i, n_atom)
        load(0, j).start()
        load(1, j).start()

    barrier = pltpu.get_barrier_semaphore()
    for partner in partners:
        pl.semaphore_signal(barrier, inc=1, device_id=(partner, atom), device_id_type=MESH)

    @pl.loop(1, n_atom)
    def _(i):
        pl.semaphore_signal(barrier, inc=1, device_id=(win, lax.rem(atom + i, n_atom)), device_id_type=MESH)

    def make_lesser(j):
        load(0, j).wait()
        load(1, j).wait()
        for i in range(own_b):
            for e in range(own_e):
                b = j * own_b + i
                g = green[e, b].reshape(2 * norb, norb)
                s = jnp.concatenate([sigma[e, b, 0], sigma[e, b, 1]], axis=1)
                product = fold(dot(g, s, (1, 0)), norb)
                lesser[e, b] = fold(dot(product, g, (1, 1)), norb).reshape(2, norb, norb)

    directions = coupling_ref.shape[0]
    out_right = [coupling_ref[d] for d in range(directions)]

    def make_part(step, j):
        for i in range(own_b):
            bent = []
            for d in range(directions):
                n = near_ref[j * own_b + i, d]
                tiles = []
                for e in range(own_e):
                    picked = lesser[e, n]
                    tiles += [picked[0], picked[1]]
                wide = dot(out_right[d], jnp.concatenate(tiles, axis=1), (1, 0)).astype(BF16)
                bent.append(
                    jnp.concatenate([wide[:, t * norb : (t + 1) * norb] for t in range(2 * own_e)], axis=0)
                )
            full = dot(jnp.concatenate(bent, axis=1), jnp.concatenate(out_right, axis=1), (1, 1)).astype(BF16)
            for e in range(own_e):
                part[step, e, i] = full[2 * e * norb : 2 * (e + 1) * norb].reshape(2, norb, norb)

    def send(k, step):
        return pltpu.make_async_remote_copy(
            src_ref=part.at[step],
            dst_ref=got.at[k, step],
            send_sem=send_sem.at[k, step],
            recv_sem=recv_sem.at[k, step],
            device_id=(partners[k], atom),
            device_id_type=MESH,
        )

    def give(step):
        return pltpu.make_async_remote_copy(
            src_ref=total.at[step],
            dst_ref=out_ref.at[pl.ds(atom * own_e, own_e)],
            send_sem=give_sem.at[step],
            recv_sem=take_sem.at[step],
            device_id=(win, owner(step)),
            device_id_type=MESH,
        )

    make_lesser(atom)
    make_lesser(lax.rem(atom + 1, n_atom))
    pl.semaphore_wait(barrier, len(bits) + n_atom - 1)

    @pl.loop(0, steps)
    def _(step):
        @pl.when(step < steps - 2)
        def _():
            make_lesser(lax.rem(atom + 2 + step, n_atom))

        make_part(step, owner(step))
        for k in range(len(bits)):
            send(k, step).start()

    weights = []
    for bit in bits:
        weight = jnp.float32(0.0)
        for mode in range(shifts_ref.shape[0]):
            weight = weight + jnp.where(shifts_ref[mode] == bit, occ_ref[mode], 0.0)
        weights.append(weight)

    def add_up(step):
        for k in range(len(bits)):
            send(k, step).wait_recv()
        for e in range(own_e):
            for i in range(own_b):
                summed = weights[0] * got[0, step, e, i].astype(F32)
                for k in range(1, len(bits)):
                    summed = summed + weights[k] * got[k, step, e, i].astype(F32)
                total[step, e, i] = summed.astype(BF16)

    @pl.loop(0, steps - 1)
    def _(step):
        add_up(step)
        give(step).start()

    add_up(steps - 1)
    own = pltpu.make_async_copy(total.at[steps - 1], out_ref.at[pl.ds(atom * own_e, own_e)], own_sem)
    own.start()

    @pl.loop(0, steps - 1)
    def _(step):
        give(step).wait()

    @pl.loop(0, steps)
    def _(step):
        for k in range(len(bits)):
            send(k, step).wait_send()

    own.wait()


def call(bits, n_atom, retarded, sigma_in, bit_shifts, occupation, neighbors, coupling):
    own_e, blocks, _, norb, _ = retarded.shape
    own_b = blocks // n_atom
    piece = (own_e, own_b, 2, norb, norb)
    count = len(bits)
    smem = pl.BlockSpec(memory_space=pltpu.SMEM)
    hbm = pl.BlockSpec(memory_space=pl.ANY)
    return pl.pallas_call(
        functools.partial(kernel, bits, n_atom),
        out_shape=jax.ShapeDtypeStruct((own_e * n_atom, own_b, 2, norb, norb), BF16),
        in_specs=[smem, smem, smem, hbm, hbm, pl.BlockSpec(memory_space=pltpu.VMEM)],
        out_specs=hbm,
        scratch_shapes=[
            pltpu.VMEM(retarded.shape, BF16),
            pltpu.VMEM(retarded.shape, BF16),
            pltpu.VMEM(retarded.shape, BF16),
            pltpu.VMEM((n_atom, *piece), BF16),
            pltpu.VMEM((count, n_atom, *piece), BF16),
            pltpu.VMEM((n_atom, *piece), BF16),
            pltpu.SemaphoreType.DMA((2, n_atom)),
            pltpu.SemaphoreType.DMA((count, n_atom)),
            pltpu.SemaphoreType.DMA((count, n_atom)),
            pltpu.SemaphoreType.DMA((n_atom,)),
            pltpu.SemaphoreType.DMA((n_atom,)),
            pltpu.SemaphoreType.DMA(()),
        ],
        compiler_params=pltpu.CompilerParams(
            collective_id=bits[1], has_side_effects=True, vmem_limit_bytes=50 * 2**20
        ),
        name="self_energy",
    )(bit_shifts, occupation, neighbors, retarded, sigma_in, coupling)


def on_device(retarded, sigma_in, bit_shifts, occupation, neighbors, coupling):
    n_atom = lax.axis_size("atom")
    top = lax.axis_size("win").bit_length() - 2
    return lax.cond(
        jnp.any(bit_shifts == 1),
        functools.partial(call, (0, 1, top), n_atom),
        functools.partial(call, (0, 2, top), n_atom),
        retarded,
        sigma_in,
        bit_shifts,
        occupation,
        neighbors,
        coupling,
    )


def solution(mesh):
    return jax.shard_map(
        on_device,
        mesh=mesh,
        in_specs=(
            P(("win", "atom"), None, None, None, None),
            P(("win", "atom"), None, None, None, None),
            P(),
            P(),
            P(),
            P(),
        ),
        out_specs=P("win", "atom", None, None, None),
        check_vma=False,
    )
```

```python
import functools

import jax
import jax.numpy as jnp
from jax import lax
from jax.experimental import pallas as pl
from jax.experimental.pallas import tpu as pltpu
from jax.sharding import PartitionSpec as P

MESH = pl.DeviceIdType.MESH
F32 = jnp.float32
BF16 = jnp.bfloat16
LAG = 3


def dot(left, right, contract):
    return lax.dot_general(left, right, ((contract[0:1], contract[1:2]), ((), ())), preferred_element_type=F32)


def fold(quad, norb):
    real = quad[:norb, :norb] - quad[norb:, norb:]
    imag = quad[:norb, norb:] + quad[norb:, :norb]
    return jnp.concatenate([real, imag], axis=0).astype(BF16)


def flip(win, bit):
    mask = 2**bit
    return win + mask * (1 - 2 * ((win // mask) % 2))


class Context:
    def __init__(self, bits, n_atom, refs):
        (
            self.shifts,
            self.occ,
            self.near,
            self.green_hbm,
            self.sigma_hbm,
            self.coupling,
            self.out,
            self.green,
            self.sigma,
            self.lesser,
            self.part,
            self.total,
            self.in_sem,
            self.give_sem,
            self.take_sem,
            self.own_sem,
        ) = refs
        self.bits = bits
        self.n_atom = n_atom
        self.own_e = self.green.shape[0]
        self.own_b = self.lesser.shape[1] // n_atom
        self.norb = self.green.shape[-1]
        self.win = lax.axis_index("win")
        self.atom = lax.axis_index("atom")

    def owner(self, step):
        return lax.rem(self.atom + 1 + step, self.n_atom)

    def load(self, kind, j):
        source, target = ((self.green_hbm, self.green), (self.sigma_hbm, self.sigma))[kind]
        rows = pl.ds(j * self.own_b, self.own_b)
        return pltpu.make_async_copy(source.at[:, rows], target.at[:, rows], self.in_sem.at[kind, j])

    def greet(self, partners):
        barrier = pltpu.get_barrier_semaphore()
        for partner in partners:
            pl.semaphore_signal(barrier, inc=1, device_id=(partner, self.atom), device_id_type=MESH)

        @pl.loop(1, self.n_atom)
        def _(i):
            peer = lax.rem(self.atom + i, self.n_atom)
            pl.semaphore_signal(barrier, inc=1, device_id=(self.win, peer), device_id_type=MESH)

        return barrier

    def start_loads(self):
        @pl.loop(0, self.n_atom)
        def _(i):
            j = lax.rem(self.atom + i, self.n_atom)
            self.load(0, j).start()
            self.load(1, j).start()

    def make_lesser(self, j):
        self.load(0, j).wait()
        self.load(1, j).wait()
        norb = self.norb
        for i in range(self.own_b):
            for e in range(self.own_e):
                b = j * self.own_b + i
                g = self.green[e, b].reshape(2 * norb, norb)
                s = jnp.concatenate([self.sigma[e, b, 0], self.sigma[e, b, 1]], axis=1)
                product = fold(dot(g, s, (1, 0)), norb)
                self.lesser[e, b] = fold(dot(product, g, (1, 1)), norb).reshape(2, norb, norb)

    def make_part(self, step):
        norb, own_e = self.norb, self.own_e
        j = self.owner(step)
        matrices = [self.coupling[d] for d in range(self.coupling.shape[0])]
        for i in range(self.own_b):
            bent = []
            for d, matrix in enumerate(matrices):
                n = self.near[j * self.own_b + i, d]
                tiles = []
                for e in range(own_e):
                    picked = self.lesser[e, n]
                    tiles += [picked[0], picked[1]]
                wide = dot(matrix, jnp.concatenate(tiles, axis=1), (1, 0)).astype(BF16)
                bent.append(
                    jnp.concatenate([wide[:, t * norb : (t + 1) * norb] for t in range(2 * own_e)], axis=0)
                )
            full = dot(jnp.concatenate(bent, axis=1), jnp.concatenate(matrices, axis=1), (1, 1)).astype(BF16)
            for e in range(own_e):
                self.part[step, e, i] = full[2 * e * norb : 2 * (e + 1) * norb].reshape(2, norb, norb)

    def make_parts(self, barrier, waits, send_part):
        steps = self.n_atom
        self.make_lesser(self.atom)
        self.make_lesser(lax.rem(self.atom + 1, self.n_atom))
        pl.semaphore_wait(barrier, waits + self.n_atom - 1)

        @pl.loop(0, steps)
        def _(step):
            @pl.when(step < steps - 2)
            def _():
                self.make_lesser(lax.rem(self.atom + 2 + step, self.n_atom))

            self.make_part(step)
            send_part(step)

    def weights(self):
        weights = []
        for bit in self.bits:
            weight = jnp.float32(0.0)
            for mode in range(self.shifts.shape[0]):
                weight = weight + jnp.where(self.shifts[mode] == bit, self.occ[mode], 0.0)
            weights.append(weight)
        return weights

    def give(self, step):
        return pltpu.make_async_remote_copy(
            src_ref=self.total.at[step],
            dst_ref=self.out.at[pl.ds(self.atom * self.own_e, self.own_e)],
            send_sem=self.give_sem.at[step],
            recv_sem=self.take_sem.at[step],
            device_id=(self.win, self.owner(step)),
            device_id_type=MESH,
        )

    def keep(self):
        last = self.n_atom - 1
        rows = pl.ds(self.atom * self.own_e, self.own_e)
        return pltpu.make_async_copy(self.total.at[last], self.out.at[rows], self.own_sem)

    def finish(self):
        @pl.loop(0, self.n_atom - 1)
        def _(step):
            self.give(step).wait()

        self.keep().wait()


def near_kernel(bits, n_atom, *refs):
    here = Context(bits, n_atom, refs[:16])
    got, send_sem, recv_sem = refs[16:]
    partners = [flip(here.win, bit) for bit in bits]
    count, steps = len(bits), n_atom

    def send(k, step):
        return pltpu.make_async_remote_copy(
            src_ref=here.part.at[step],
            dst_ref=got.at[k, step],
            send_sem=send_sem.at[k, step],
            recv_sem=recv_sem.at[k, step],
            device_id=(partners[k], here.atom),
            device_id_type=MESH,
        )

    def send_part(step):
        for k in range(count):
            send(k, step).start()

    here.start_loads()
    barrier = here.greet(partners)
    here.make_parts(barrier, count, send_part)
    weights = here.weights()

    def add_up(step):
        for k in range(count):
            send(k, step).wait_recv()
        for e in range(here.own_e):
            for i in range(here.own_b):
                summed = weights[0] * got[0, step, e, i].astype(F32)
                for k in range(1, count):
                    summed = summed + weights[k] * got[k, step, e, i].astype(F32)
                here.total[step, e, i] = summed.astype(BF16)

    @pl.loop(0, steps - 1)
    def _(step):
        add_up(step)
        here.give(step).start()

    add_up(steps - 1)
    here.keep().start()

    @pl.loop(0, steps)
    def _(step):
        for k in range(count):
            send(k, step).wait_send()

    here.finish()


def far_kernel(bits, n_atom, *refs):
    here = Context(bits, n_atom, refs[:16])
    got_first, got_away, got_on, got_sum, got_top, mixed, half_send, half_recv, top_send, top_recv = refs[16:]
    steps = n_atom
    half = here.own_e // 2
    lead, rest = pl.ds(0, half), pl.ds(half, half)
    twin = flip(here.win, bits[0])
    cross = flip(twin, bits[1])
    across = flip(here.win, bits[2])

    def hop(kind, step):
        source, target, win = (
            (here.part.at[step, lead], got_first.at[step], twin),
            (here.part.at[step, rest], got_away.at[step], cross),
            (got_first.at[step], got_on.at[step], cross),
            (mixed.at[step], got_sum.at[step], twin),
        )[kind]
        return pltpu.make_async_remote_copy(
            src_ref=source,
            dst_ref=target,
            send_sem=half_send.at[kind, step],
            recv_sem=half_recv.at[kind, step],
            device_id=(win, here.atom),
            device_id_type=MESH,
        )

    def top(step):
        return pltpu.make_async_remote_copy(
            src_ref=here.part.at[step],
            dst_ref=got_top.at[step],
            send_sem=top_send.at[step],
            recv_sem=top_recv.at[step],
            device_id=(across, here.atom),
            device_id_type=MESH,
        )

    def send_part(step):
        hop(0, step).start()
        hop(1, step).start()
        top(step).start()

    here.start_loads()
    barrier = here.greet([twin, cross, across])
    here.make_parts(barrier, 3, send_part)
    low, mid, high = here.weights()

    def pass_on(step):
        hop(0, step).wait_recv()
        hop(2, step).start()
        hop(1, step).wait_recv()
        for e in range(half):
            for i in range(here.own_b):
                summed = low * here.part[step, half + e, i].astype(F32) + mid * got_away[step, e, i].astype(F32)
                mixed[step, e, i] = summed.astype(BF16)
        hop(3, step).start()

    def add_up(step):
        hop(2, step).wait_recv()
        hop(3, step).wait_recv()
        top(step).wait_recv()
        for e in range(half):
            for i in range(here.own_b):
                summed = low * got_first[step, e, i].astype(F32) + mid * got_on[step, e, i].astype(F32)
                summed = summed + high * got_top[step, e, i].astype(F32)
                here.total[step, e, i] = summed.astype(BF16)
                summed = got_sum[step, e, i].astype(F32) + high * got_top[step, half + e, i].astype(F32)
                here.total[step, half + e, i] = summed.astype(BF16)

    lag = min(LAG, steps)

    @pl.loop(0, lag)
    def _(step):
        pass_on(step)

    @pl.loop(lag, steps)
    def _(step):
        pass_on(step)
        add_up(step - lag)
        here.give(step - lag).start()

    @pl.loop(steps - lag, steps - 1)
    def _(step):
        add_up(step)
        here.give(step).start()

    add_up(steps - 1)
    here.keep().start()

    @pl.loop(0, steps)
    def _(step):
        for kind in range(4):
            hop(kind, step).wait_send()
        top(step).wait_send()

    here.finish()


def call(bits, n_atom, retarded, sigma_in, bit_shifts, occupation, neighbors, coupling):
    own_e, blocks, _, norb, _ = retarded.shape
    own_b = blocks // n_atom
    pieces = (n_atom, own_e, own_b, 2, norb, norb)
    halves = (n_atom, own_e // 2, own_b, 2, norb, norb)
    count = len(bits)
    smem = pl.BlockSpec(memory_space=pltpu.SMEM)
    hbm = pl.BlockSpec(memory_space=pl.ANY)
    dma = pltpu.SemaphoreType.DMA
    if bits[1] == 1:
        body = near_kernel
        extra = [pltpu.VMEM((count, *pieces), BF16), dma((count, n_atom)), dma((count, n_atom))]
    else:
        body = far_kernel
        extra = [pltpu.VMEM(halves, BF16) for _ in range(4)]
        extra += [pltpu.VMEM(pieces, BF16), pltpu.VMEM(halves, BF16)]
        extra += [dma((4, n_atom)), dma((4, n_atom)), dma((n_atom,)), dma((n_atom,))]
    return pl.pallas_call(
        functools.partial(body, bits, n_atom),
        out_shape=jax.ShapeDtypeStruct((own_e * n_atom, own_b, 2, norb, norb), BF16),
        in_specs=[smem, smem, smem, hbm, hbm, pl.BlockSpec(memory_space=pltpu.VMEM)],
        out_specs=hbm,
        scratch_shapes=[
            pltpu.VMEM(retarded.shape, BF16),
            pltpu.VMEM(retarded.shape, BF16),
            pltpu.VMEM(retarded.shape, BF16),
            pltpu.VMEM(pieces, BF16),
            pltpu.VMEM(pieces, BF16),
            dma((2, n_atom)),
            dma((n_atom,)),
            dma((n_atom,)),
            dma(()),
            *extra,
        ],
        compiler_params=pltpu.CompilerParams(
            collective_id=bits[1], has_side_effects=True, vmem_limit_bytes=50 * 2**20
        ),
        name="self_energy",
    )(bit_shifts, occupation, neighbors, retarded, sigma_in, coupling)


def on_device(retarded, sigma_in, bit_shifts, occupation, neighbors, coupling):
    n_atom = lax.axis_size("atom")
    top = lax.axis_size("win").bit_length() - 2
    return lax.cond(
        jnp.any(bit_shifts == 1),
        functools.partial(call, (0, 1, top), n_atom),
        functools.partial(call, (0, 2, top), n_atom),
        retarded,
        sigma_in,
        bit_shifts,
        occupation,
        neighbors,
        coupling,
    )


def solution(mesh):
    return jax.shard_map(
        on_device,
        mesh=mesh,
        in_specs=(
            P(("win", "atom"), None, None, None, None),
            P(("win", "atom"), None, None, None, None),
            P(),
            P(),
            P(),
            P(),
        ),
        out_specs=P("win", "atom", None, None, None),
        check_vma=False,
    )
```

```python
import functools

import jax
import jax.numpy as jnp
from jax import lax
from jax.experimental import pallas as pl
from jax.experimental.pallas import tpu as pltpu
from jax.sharding import PartitionSpec as P

MESH = pl.DeviceIdType.MESH
F32 = jnp.float32
BF16 = jnp.bfloat16
LAG = 3
STRIDE = 3


def dot(left, right, contract):
    return lax.dot_general(left, right, ((contract[0:1], contract[1:2]), ((), ())), preferred_element_type=F32)


def fold(quad, norb):
    real = quad[:norb, :norb] - quad[norb:, norb:]
    imag = quad[:norb, norb:] + quad[norb:, :norb]
    return jnp.concatenate([real, imag], axis=0).astype(BF16)


def flip(win, bit):
    mask = 2**bit
    return win + mask * (1 - 2 * ((win // mask) % 2))


class Context:
    def __init__(self, bits, n_atom, refs):
        (
            self.shifts_hbm,
            self.occ_hbm,
            self.near_hbm,
            self.green_hbm,
            self.sigma_hbm,
            self.coupling_hbm,
            self.out,
            self.shifts,
            self.occ,
            self.near,
            self.coupling,
            self.green,
            self.sigma,
            self.lesser,
            self.part,
            self.held,
            self.small_sem,
            self.in_sem,
            self.give_sem,
            self.take_sem,
        ) = refs
        self.bits = bits
        self.n_atom = n_atom
        self.own_e = self.green.shape[0]
        self.blocks = self.lesser.shape[1]
        self.own_b = self.blocks // n_atom
        self.norb = self.green.shape[-1]
        self.win = lax.axis_index("win")
        self.atom = lax.axis_index("atom")
        self.sign = 1 - 2 * (self.atom % 2)

    def owner(self, offset):
        return lax.rem(self.atom + offset, self.n_atom)

    def sent(self, turn):
        return lax.rem(self.sign * ((STRIDE * turn) % self.n_atom) + self.n_atom, self.n_atom)

    def met(self, turn):
        offset = (STRIDE * turn) % self.n_atom
        return lax.rem(self.sign * (1 - 2 * (offset % 2)) * offset + self.n_atom, self.n_atom)

    def block(self, place):
        return lax.rem(self.atom * self.own_b + place + self.blocks - 1, self.blocks)

    def small(self, which):
        source, target = (
            (self.near_hbm, self.near),
            (self.coupling_hbm, self.coupling),
            (self.shifts_hbm, self.shifts),
            (self.occ_hbm, self.occ),
        )[which]
        return pltpu.make_async_copy(source, target, self.small_sem.at[which])

    def load(self, kind, place):
        source, target = ((self.green_hbm, self.green), (self.sigma_hbm, self.sigma))[kind]
        b = self.block(place)
        return pltpu.make_async_copy(source.at[:, b], target.at[:, b], self.in_sem.at[kind, place])

    def start_loads(self, places):
        @pl.loop(*places)
        def _(place):
            self.load(0, place).start()
            self.load(1, place).start()

    def begin(self, partners):
        first = self.own_b + 2
        self.start_loads((0, first))
        for which in range(4):
            self.small(which).start()
        barrier = pltpu.get_barrier_semaphore()
        for partner in partners:
            pl.semaphore_signal(barrier, inc=1, device_id=(partner, self.atom), device_id_type=MESH)

        @pl.loop(1, self.n_atom)
        def _(i):
            pl.semaphore_signal(barrier, inc=1, device_id=(self.win, self.owner(i)), device_id_type=MESH)

        self.start_loads((first, self.blocks))
        for place in range(first):
            self.make_lesser(place)
        self.small(0).wait()
        self.small(1).wait()
        self.make_part(0, self.held)
        pl.semaphore_wait(barrier, len(partners) + self.n_atom - 1)

    def make_lesser(self, place):
        self.load(0, place).wait()
        self.load(1, place).wait()
        norb, b = self.norb, self.block(place)
        for e in range(self.own_e):
            g = self.green[e, b].reshape(2 * norb, norb)
            s = jnp.concatenate([self.sigma[e, b, 0], self.sigma[e, b, 1]], axis=1)
            product = fold(dot(g, s, (1, 0)), norb)
            self.lesser[e, b] = fold(dot(product, g, (1, 1)), norb).reshape(2, norb, norb)

    def make_part(self, step, target):
        norb, own_e = self.norb, self.own_e
        j = self.owner(step)
        matrices = [self.coupling[d] for d in range(self.coupling.shape[0])]
        for i in range(self.own_b):
            bent = []
            for d, matrix in enumerate(matrices):
                n = self.near[d, j * self.own_b + i]
                tiles = []
                for e in range(own_e):
                    picked = self.lesser[e, n]
                    tiles += [picked[0], picked[1]]
                wide = dot(matrix, jnp.concatenate(tiles, axis=1), (1, 0)).astype(BF16)
                bent.append(
                    jnp.concatenate([wide[:, t * norb : (t + 1) * norb] for t in range(2 * own_e)], axis=0)
                )
            full = dot(jnp.concatenate(bent, axis=1), jnp.concatenate(matrices, axis=1), (1, 1)).astype(BF16)
            for e in range(own_e):
                target[step, e, i] = full[2 * e * norb : 2 * (e + 1) * norb].reshape(2, norb, norb)

    def give(self, step):
        return pltpu.make_async_remote_copy(
            src_ref=self.part.at[step],
            dst_ref=self.held.at[step],
            send_sem=self.give_sem.at[step],
            recv_sem=self.take_sem.at[step],
            device_id=(self.win, self.owner(step)),
            device_id_type=MESH,
        )

    def make_parts(self, send):
        steps = self.n_atom
        lag = min(LAG, steps - 1)
        apart = self.sign * pow(STRIDE, -1, steps) + steps
        send(0)

        @pl.loop(1, steps)
        def _(turn):
            offset = self.sent(turn)

            @pl.when((turn + 2 * steps - apart) % steps > turn)
            def _():
                for i in range(self.own_b):
                    self.make_lesser(self.own_b * offset + i)

            @pl.when((turn + apart) % steps > turn)
            def _():
                for i in range(self.own_b):
                    self.make_lesser(self.own_b * (offset + 1) + i)

            self.make_part(offset, self.part)
            self.give(offset).start()

            @pl.when(turn > lag)
            def _():
                self.send_held(self.met(turn - lag), send)

        @pl.loop(steps - lag, steps)
        def _(turn):
            self.send_held(self.met(turn), send)

    def send_held(self, slot, send):
        self.give(slot).wait_recv()
        send(slot)

    def weights(self):
        self.small(2).wait()
        self.small(3).wait()
        weights = []
        for bit in self.bits:
            weight = jnp.float32(0.0)
            for mode in range(self.shifts.shape[0]):
                weight = weight + jnp.where(self.shifts[mode] == bit, self.occ[mode], 0.0)
            weights.append(weight)
        return weights

    def store(self, slot, e, i, value):
        sender = lax.rem(self.atom + self.n_atom - slot, self.n_atom)
        self.out[sender * self.own_e + e, i] = value.astype(BF16)

    def finish(self):
        @pl.loop(1, self.n_atom)
        def _(step):
            self.give(step).wait_send()


def near_kernel(bits, n_atom, *refs):
    here = Context(bits, n_atom, refs[:20])
    got, send_sem, recv_sem = refs[20:]
    partners = [flip(here.win, bit) for bit in bits]
    count = len(bits)

    def pass_to(k, slot):
        return pltpu.make_async_remote_copy(
            src_ref=here.held.at[slot],
            dst_ref=got.at[k, slot],
            send_sem=send_sem.at[k, slot],
            recv_sem=recv_sem.at[k, slot],
            device_id=(partners[k], here.atom),
            device_id_type=MESH,
        )

    def send(slot):
        for k in range(count):
            pass_to(k, slot).start()

    here.begin(partners)
    here.make_parts(send)
    weights = here.weights()

    @pl.loop(0, n_atom)
    def _(turn):
        slot = here.met(turn)
        for k in range(count):
            pass_to(k, slot).wait_recv()
        for e in range(here.own_e):
            for i in range(here.own_b):
                summed = weights[0] * got[0, slot, e, i].astype(F32)
                for k in range(1, count):
                    summed = summed + weights[k] * got[k, slot, e, i].astype(F32)
                here.store(slot, e, i, summed)

    @pl.loop(0, n_atom)
    def _(slot):
        for k in range(count):
            pass_to(k, slot).wait_send()

    here.finish()


def far_kernel(bits, n_atom, *refs):
    here = Context(bits, n_atom, refs[:20])
    got_first, got_away, got_on, got_sum, got_top, mixed, half_send, half_recv, top_send, top_recv = refs[20:]
    half = here.own_e // 2
    lead, rest = pl.ds(0, half), pl.ds(half, half)
    twin = flip(here.win, bits[0])
    cross = flip(twin, bits[1])
    across = flip(here.win, bits[2])

    def hop(kind, slot):
        source, target, win = (
            (here.held.at[slot, lead], got_first.at[slot], twin),
            (here.held.at[slot, rest], got_away.at[slot], cross),
            (got_first.at[slot], got_on.at[slot], cross),
            (mixed.at[slot], got_sum.at[slot], twin),
        )[kind]
        return pltpu.make_async_remote_copy(
            src_ref=source,
            dst_ref=target,
            send_sem=half_send.at[kind, slot],
            recv_sem=half_recv.at[kind, slot],
            device_id=(win, here.atom),
            device_id_type=MESH,
        )

    def top(slot):
        return pltpu.make_async_remote_copy(
            src_ref=here.held.at[slot],
            dst_ref=got_top.at[slot],
            send_sem=top_send.at[slot],
            recv_sem=top_recv.at[slot],
            device_id=(across, here.atom),
            device_id_type=MESH,
        )

    def send(slot):
        hop(0, slot).start()
        hop(1, slot).start()

    here.begin([twin, cross, across])
    here.make_parts(send)
    low, mid, high = here.weights()

    def pass_on(slot):
        hop(0, slot).wait_recv()
        hop(2, slot).start()
        top(slot).start()
        hop(1, slot).wait_recv()
        for e in range(half):
            for i in range(here.own_b):
                summed = low * here.held[slot, half + e, i].astype(F32) + mid * got_away[slot, e, i].astype(F32)
                mixed[slot, e, i] = summed.astype(BF16)
        hop(3, slot).start()

    @pl.loop(0, n_atom)
    def _(turn):
        pass_on(here.met(turn))

    @pl.loop(0, n_atom)
    def _(turn):
        slot = here.met(turn)
        hop(2, slot).wait_recv()
        hop(3, slot).wait_recv()
        top(slot).wait_recv()
        for e in range(half):
            for i in range(here.own_b):
                summed = low * got_first[slot, e, i].astype(F32) + mid * got_on[slot, e, i].astype(F32)
                here.store(slot, e, i, summed + high * got_top[slot, e, i].astype(F32))
                summed = got_sum[slot, e, i].astype(F32) + high * got_top[slot, half + e, i].astype(F32)
                here.store(slot, half + e, i, summed)

    @pl.loop(0, n_atom)
    def _(slot):
        for kind in range(4):
            hop(kind, slot).wait_send()
        top(slot).wait_send()

    here.finish()


def call(bits, n_atom, retarded, sigma_in, bit_shifts, occupation, neighbors, coupling):
    own_e, blocks, _, norb, _ = retarded.shape
    own_b = blocks // n_atom
    pieces = (n_atom, own_e, own_b, 2, norb, norb)
    halves = (n_atom, own_e // 2, own_b, 2, norb, norb)
    count = len(bits)
    dma = pltpu.SemaphoreType.DMA
    if bits[1] == 1:
        body = near_kernel
        extra = [pltpu.VMEM((count, *pieces), BF16), dma((count, n_atom)), dma((count, n_atom))]
    else:
        body = far_kernel
        extra = [pltpu.VMEM(halves, BF16) for _ in range(4)]
        extra += [pltpu.VMEM(pieces, BF16), pltpu.VMEM(halves, BF16)]
        extra += [dma((4, n_atom)), dma((4, n_atom)), dma((n_atom,)), dma((n_atom,))]
    return pl.pallas_call(
        functools.partial(body, bits, n_atom),
        out_shape=jax.ShapeDtypeStruct((own_e * n_atom, own_b, 2, norb, norb), BF16),
        in_specs=[pl.BlockSpec(memory_space=pl.ANY)] * 6,
        out_specs=pl.BlockSpec(memory_space=pltpu.VMEM),
        scratch_shapes=[
            pltpu.SMEM(bit_shifts.shape, jnp.int32),
            pltpu.SMEM(occupation.shape, F32),
            pltpu.SMEM(neighbors.shape[::-1], jnp.int32),
            pltpu.VMEM(coupling.shape, BF16),
            pltpu.VMEM(retarded.shape, BF16),
            pltpu.VMEM(retarded.shape, BF16),
            pltpu.VMEM(retarded.shape, BF16),
            pltpu.VMEM(pieces, BF16),
            pltpu.VMEM(pieces, BF16),
            dma((4,)),
            dma((2, blocks)),
            dma((n_atom,)),
            dma((n_atom,)),
            *extra,
        ],
        compiler_params=pltpu.CompilerParams(
            collective_id=bits[1], has_side_effects=True, vmem_limit_bytes=50 * 2**20
        ),
        name="self_energy",
    )(bit_shifts, occupation, neighbors.T, retarded, sigma_in, coupling)


def on_device(retarded, sigma_in, bit_shifts, occupation, neighbors, coupling):
    n_atom = lax.axis_size("atom")
    top = lax.axis_size("win").bit_length() - 2
    return lax.cond(
        jnp.any(bit_shifts == 1),
        functools.partial(call, (0, 1, top), n_atom),
        functools.partial(call, (0, 2, top), n_atom),
        retarded,
        sigma_in,
        bit_shifts,
        occupation,
        neighbors,
        coupling,
    )


def solution(mesh):
    return jax.shard_map(
        on_device,
        mesh=mesh,
        in_specs=(
            P(("win", "atom"), None, None, None, None),
            P(("win", "atom"), None, None, None, None),
            P(),
            P(),
            P(),
            P(),
        ),
        out_specs=P("win", "atom", None, None, None),
        check_vma=False,
    )
```

```python
import functools

import jax
import jax.numpy as jnp
from jax import lax
from jax.experimental import pallas as pl
from jax.experimental.pallas import tpu as pltpu
from jax.sharding import PartitionSpec as P

MESH = pl.DeviceIdType.MESH
F32 = jnp.float32
BF16 = jnp.bfloat16
LAG = 2
STRIDE = 3


def dot(left, right, contract):
    return lax.dot_general(left, right, ((contract[0:1], contract[1:2]), ((), ())), preferred_element_type=F32)


def fold(quad, norb):
    real = quad[:norb, :norb] - quad[norb:, norb:]
    imag = quad[:norb, norb:] + quad[norb:, :norb]
    return jnp.concatenate([real, imag], axis=0).astype(BF16)


def flip(win, bit):
    mask = 2**bit
    return win + mask * (1 - 2 * ((win // mask) % 2))


class Context:
    def __init__(self, bits, n_atom, refs):
        (
            self.shifts_hbm,
            self.occ_hbm,
            self.near_hbm,
            self.green_hbm,
            self.sigma_hbm,
            self.coupling_hbm,
            self.out,
            self.shifts,
            self.occ,
            self.near,
            self.coupling,
            self.green,
            self.sigma,
            self.lesser,
            self.part,
            self.held,
            self.small_sem,
            self.in_sem,
            self.give_sem,
            self.take_sem,
        ) = refs
        self.bits = bits
        self.n_atom = n_atom
        self.own_e = self.green.shape[0]
        self.blocks = self.lesser.shape[1]
        self.own_b = self.blocks // n_atom
        self.norb = self.green.shape[-1]
        self.win = lax.axis_index("win")
        self.atom = lax.axis_index("atom")
        self.sign = 1 - 2 * (self.atom % 2)

    def owner(self, offset):
        return lax.rem(self.atom + offset, self.n_atom)

    def swapped(self, value):
        other = STRIDE % self.n_atom
        return jnp.where(value == 1, other, jnp.where(value == other, 1, value))

    def distance(self, turn):
        return self.swapped((STRIDE * turn) % self.n_atom)

    def turn_of(self, distance):
        return (pow(STRIDE, -1, self.n_atom) * self.swapped(distance)) % self.n_atom

    def sent(self, turn):
        return lax.rem(self.sign * self.distance(turn) + self.n_atom, self.n_atom)

    def met(self, turn):
        distance = self.distance(turn)
        return lax.rem(self.sign * (1 - 2 * (distance % 2)) * distance + self.n_atom, self.n_atom)

    def block(self, place):
        return lax.rem(self.atom * self.own_b + place + self.blocks - 1, self.blocks)

    def small(self, which):
        source, target = (
            (self.near_hbm, self.near),
            (self.coupling_hbm, self.coupling),
            (self.shifts_hbm, self.shifts),
            (self.occ_hbm, self.occ),
        )[which]
        return pltpu.make_async_copy(source, target, self.small_sem.at[which])

    def load(self, kind, place):
        source, target = ((self.green_hbm, self.green), (self.sigma_hbm, self.sigma))[kind]
        b = self.block(place)
        return pltpu.make_async_copy(source.at[:, b], target.at[:, b], self.in_sem.at[kind, place])

    def start_loads(self, places):
        @pl.loop(*places)
        def _(place):
            self.load(0, place).start()
            self.load(1, place).start()

    def begin(self, partners, send):
        first = self.own_b + 2
        self.start_loads((0, first))
        for which in range(4):
            self.small(which).start()
        barrier = pltpu.get_barrier_semaphore()
        for partner in partners:
            pl.semaphore_signal(barrier, inc=1, device_id=(partner, self.atom), device_id_type=MESH)

        @pl.loop(1, self.n_atom)
        def _(i):
            pl.semaphore_signal(barrier, inc=1, device_id=(self.win, self.owner(i)), device_id_type=MESH)

        early = self.n_atom > 2
        forward = (self.sign + 1) // 2
        if early:
            start = self.own_b * (2 * forward + (self.n_atom - 1) * (1 - forward))
            self.start_loads((start, start + self.own_b))
        for place in range(first):
            self.make_lesser(place)
        self.small(0).wait()
        self.small(1).wait()
        self.make_part(0, self.held)
        pl.semaphore_wait(barrier, len(partners) + self.n_atom - 1)
        send(0)
        if early:
            start = first + self.own_b * forward
            self.start_loads((start, start + self.blocks - first - self.own_b))

    def make_lesser(self, place):
        self.load(0, place).wait()
        self.load(1, place).wait()
        norb, b = self.norb, self.block(place)
        for e in range(self.own_e):
            g = self.green[e, b].reshape(2 * norb, norb)
            s = jnp.concatenate([self.sigma[e, b, 0], self.sigma[e, b, 1]], axis=1)
            product = fold(dot(g, s, (1, 0)), norb)
            self.lesser[e, b] = fold(dot(product, g, (1, 1)), norb).reshape(2, norb, norb)

    def make_part(self, step, target):
        norb, own_e = self.norb, self.own_e
        j = self.owner(step)
        matrices = [self.coupling[d] for d in range(self.coupling.shape[0])]
        for i in range(self.own_b):
            bent = []
            for d, matrix in enumerate(matrices):
                n = self.near[d, j * self.own_b + i]
                tiles = []
                for e in range(own_e):
                    picked = self.lesser[e, n]
                    tiles += [picked[0], picked[1]]
                wide = dot(matrix, jnp.concatenate(tiles, axis=1), (1, 0)).astype(BF16)
                bent.append(
                    jnp.concatenate([wide[:, t * norb : (t + 1) * norb] for t in range(2 * own_e)], axis=0)
                )
            full = dot(jnp.concatenate(bent, axis=1), jnp.concatenate(matrices, axis=1), (1, 1)).astype(BF16)
            for e in range(own_e):
                target[step, e, i] = full[2 * e * norb : 2 * (e + 1) * norb].reshape(2, norb, norb)

    def give(self, step):
        return pltpu.make_async_remote_copy(
            src_ref=self.part.at[step],
            dst_ref=self.held.at[step],
            send_sem=self.give_sem.at[step],
            recv_sem=self.take_sem.at[step],
            device_id=(self.win, self.owner(step)),
            device_id_type=MESH,
        )

    def make_parts(self, send):
        steps = self.n_atom
        lag = min(LAG, steps - 1)

        @pl.loop(1, steps)
        def _(turn):
            offset = self.sent(turn)

            before = self.turn_of((self.distance(turn) + steps - self.sign) % steps)
            after = self.turn_of((self.distance(turn) + steps + self.sign) % steps)

            @pl.when(before > turn)
            def _():
                for i in range(self.own_b):
                    self.make_lesser(self.own_b * offset + i)

            @pl.when(after > turn)
            def _():
                for i in range(self.own_b):
                    self.make_lesser(self.own_b * (offset + 1) + i)

            self.make_part(offset, self.part)
            self.give(offset).start()

            @pl.when(turn == 2)
            def _():
                self.send_held(self.met(1), send)

            @pl.when(turn > lag + 1)
            def _():
                self.send_held(self.met(turn - lag), send)

        @pl.loop(steps - lag, steps)
        def _(turn):
            self.send_held(self.met(turn), send)

    def send_held(self, slot, send):
        self.give(slot).wait_recv()
        send(slot)

    def weights(self):
        self.small(2).wait()
        self.small(3).wait()
        weights = []
        for bit in self.bits:
            weight = jnp.float32(0.0)
            for mode in range(self.shifts.shape[0]):
                weight = weight + jnp.where(self.shifts[mode] == bit, self.occ[mode], 0.0)
            weights.append(weight)
        return weights

    def store(self, slot, e, i, value):
        sender = lax.rem(self.atom + self.n_atom - slot, self.n_atom)
        self.out[sender * self.own_e + e, i] = value.astype(BF16)

    def finish(self):
        @pl.loop(1, self.n_atom)
        def _(step):
            self.give(step).wait_send()


def near_kernel(bits, n_atom, *refs):
    here = Context(bits, n_atom, refs[:20])
    got, send_sem, recv_sem = refs[20:]
    partners = [flip(here.win, bit) for bit in bits]
    count = len(bits)

    def pass_to(k, slot):
        return pltpu.make_async_remote_copy(
            src_ref=here.held.at[slot],
            dst_ref=got.at[k, slot],
            send_sem=send_sem.at[k, slot],
            recv_sem=recv_sem.at[k, slot],
            device_id=(partners[k], here.atom),
            device_id_type=MESH,
        )

    def send(slot):
        for k in range(count):
            pass_to(k, slot).start()

    here.begin(partners, send)
    here.make_parts(send)
    weights = here.weights()

    @pl.loop(0, n_atom)
    def _(turn):
        slot = here.met(turn)
        for k in range(count):
            pass_to(k, slot).wait_recv()
        for e in range(here.own_e):
            for i in range(here.own_b):
                summed = weights[0] * got[0, slot, e, i].astype(F32)
                for k in range(1, count):
                    summed = summed + weights[k] * got[k, slot, e, i].astype(F32)
                here.store(slot, e, i, summed)

    @pl.loop(0, n_atom)
    def _(slot):
        for k in range(count):
            pass_to(k, slot).wait_send()

    here.finish()


def far_kernel(bits, n_atom, *refs):
    here = Context(bits, n_atom, refs[:20])
    got_first, got_away, got_on, got_sum, got_top, mixed, half_send, half_recv, top_send, top_recv = refs[20:]
    half = here.own_e // 2
    lead, rest = pl.ds(0, half), pl.ds(half, half)
    twin = flip(here.win, bits[0])
    cross = flip(twin, bits[1])
    across = flip(here.win, bits[2])

    def hop(kind, slot):
        source, target, win = (
            (here.held.at[slot, lead], got_first.at[slot], twin),
            (here.held.at[slot, rest], got_away.at[slot], cross),
            (got_first.at[slot], got_on.at[slot], cross),
            (mixed.at[slot], got_sum.at[slot], twin),
        )[kind]
        return pltpu.make_async_remote_copy(
            src_ref=source,
            dst_ref=target,
            send_sem=half_send.at[kind, slot],
            recv_sem=half_recv.at[kind, slot],
            device_id=(win, here.atom),
            device_id_type=MESH,
        )

    def top(slot):
        return pltpu.make_async_remote_copy(
            src_ref=here.held.at[slot],
            dst_ref=got_top.at[slot],
            send_sem=top_send.at[slot],
            recv_sem=top_recv.at[slot],
            device_id=(across, here.atom),
            device_id_type=MESH,
        )

    def send(slot):
        hop(0, slot).start()
        hop(1, slot).start()

    here.begin([twin, cross, across], send)
    here.make_parts(send)
    low, mid, high = here.weights()

    def pass_on(slot):
        hop(0, slot).wait_recv()
        hop(2, slot).start()
        top(slot).start()
        hop(1, slot).wait_recv()
        for e in range(half):
            for i in range(here.own_b):
                summed = low * here.held[slot, half + e, i].astype(F32) + mid * got_away[slot, e, i].astype(F32)
                mixed[slot, e, i] = summed.astype(BF16)
        hop(3, slot).start()

    @pl.loop(0, n_atom)
    def _(turn):
        pass_on(here.met(turn))

    @pl.loop(0, n_atom)
    def _(turn):
        slot = here.met(turn)
        hop(2, slot).wait_recv()
        hop(3, slot).wait_recv()
        top(slot).wait_recv()
        for e in range(half):
            for i in range(here.own_b):
                summed = low * got_first[slot, e, i].astype(F32) + mid * got_on[slot, e, i].astype(F32)
                here.store(slot, e, i, summed + high * got_top[slot, e, i].astype(F32))
                summed = got_sum[slot, e, i].astype(F32) + high * got_top[slot, half + e, i].astype(F32)
                here.store(slot, half + e, i, summed)

    @pl.loop(0, n_atom)
    def _(slot):
        for kind in range(4):
            hop(kind, slot).wait_send()
        top(slot).wait_send()

    here.finish()


def call(bits, n_atom, retarded, sigma_in, bit_shifts, occupation, neighbors, coupling):
    own_e, blocks, _, norb, _ = retarded.shape
    own_b = blocks // n_atom
    pieces = (n_atom, own_e, own_b, 2, norb, norb)
    halves = (n_atom, own_e // 2, own_b, 2, norb, norb)
    count = len(bits)
    dma = pltpu.SemaphoreType.DMA
    if bits[1] == 1:
        body = near_kernel
        extra = [pltpu.VMEM((count, *pieces), BF16), dma((count, n_atom)), dma((count, n_atom))]
    else:
        body = far_kernel
        extra = [pltpu.VMEM(halves, BF16) for _ in range(4)]
        extra += [pltpu.VMEM(pieces, BF16), pltpu.VMEM(halves, BF16)]
        extra += [dma((4, n_atom)), dma((4, n_atom)), dma((n_atom,)), dma((n_atom,))]
    return pl.pallas_call(
        functools.partial(body, bits, n_atom),
        out_shape=jax.ShapeDtypeStruct((own_e * n_atom, own_b, 2, norb, norb), BF16),
        in_specs=[pl.BlockSpec(memory_space=pl.ANY)] * 6,
        out_specs=pl.BlockSpec(memory_space=pltpu.VMEM),
        scratch_shapes=[
            pltpu.SMEM(bit_shifts.shape, jnp.int32),
            pltpu.SMEM(occupation.shape, F32),
            pltpu.SMEM(neighbors.shape[::-1], jnp.int32),
            pltpu.VMEM(coupling.shape, BF16),
            pltpu.VMEM(retarded.shape, BF16),
            pltpu.VMEM(retarded.shape, BF16),
            pltpu.VMEM(retarded.shape, BF16),
            pltpu.VMEM(pieces, BF16),
            pltpu.VMEM(pieces, BF16),
            dma((4,)),
            dma((2, blocks)),
            dma((n_atom,)),
            dma((n_atom,)),
            *extra,
        ],
        compiler_params=pltpu.CompilerParams(
            collective_id=bits[1], has_side_effects=True, vmem_limit_bytes=50 * 2**20
        ),
        name="self_energy",
    )(bit_shifts, occupation, neighbors.T, retarded, sigma_in, coupling)


def on_device(retarded, sigma_in, bit_shifts, occupation, neighbors, coupling):
    n_atom = lax.axis_size("atom")
    top = lax.axis_size("win").bit_length() - 2
    return lax.cond(
        jnp.any(bit_shifts == 1),
        functools.partial(call, (0, 1, top), n_atom),
        functools.partial(call, (0, 2, top), n_atom),
        retarded,
        sigma_in,
        bit_shifts,
        occupation,
        neighbors,
        coupling,
    )


def solution(mesh):
    return jax.shard_map(
        on_device,
        mesh=mesh,
        in_specs=(
            P(("win", "atom"), None, None, None, None),
            P(("win", "atom"), None, None, None, None),
            P(),
            P(),
            P(),
            P(),
        ),
        out_specs=P("win", "atom", None, None, None),
        check_vma=False,
    )
```

```python
import functools

import jax
import jax.numpy as jnp
from jax import lax
from jax.experimental import pallas as pl
from jax.experimental.pallas import tpu as pltpu
from jax.sharding import PartitionSpec as P

MESH = pl.DeviceIdType.MESH
F32 = jnp.float32
BF16 = jnp.bfloat16
LAG = 2
STRIDE = 3


def dot(left, right, contract):
    return lax.dot_general(left, right, ((contract[0:1], contract[1:2]), ((), ())), preferred_element_type=F32)


def fold(quad, norb):
    real = quad[:norb, :norb] - quad[norb:, norb:]
    imag = quad[:norb, norb:] + quad[norb:, :norb]
    return jnp.concatenate([real, imag], axis=0).astype(BF16)


def flip(win, bit):
    mask = 2**bit
    return win + mask * (1 - 2 * ((win // mask) % 2))


class Context:
    def __init__(self, bits, n_atom, refs):
        (
            self.shifts_hbm,
            self.occ_hbm,
            self.near_hbm,
            self.green_hbm,
            self.sigma_hbm,
            self.coupling_hbm,
            self.out,
            self.shifts,
            self.occ,
            self.near,
            self.coupling,
            self.green,
            self.sigma,
            self.lesser,
            self.part,
            self.held,
            self.small_sem,
            self.in_sem,
            self.give_sem,
            self.take_sem,
        ) = refs
        self.bits = bits
        self.n_atom = n_atom
        self.own_e = self.green.shape[0]
        self.blocks = self.lesser.shape[1]
        self.own_b = self.blocks // n_atom
        self.norb = self.green.shape[-1]
        self.win = lax.axis_index("win")
        self.atom = lax.axis_index("atom")
        self.sign = 1 - 2 * (self.atom % 2)

    def owner(self, offset):
        return lax.rem(self.atom + offset, self.n_atom)

    def swapped(self, value):
        other = STRIDE % self.n_atom
        return jnp.where(value == 1, other, jnp.where(value == other, 1, value))

    def distance(self, turn):
        return self.swapped((STRIDE * turn) % self.n_atom)

    def turn_of(self, distance):
        return (pow(STRIDE, -1, self.n_atom) * self.swapped(distance)) % self.n_atom

    def sent(self, turn):
        return lax.rem(self.sign * self.distance(turn) + self.n_atom, self.n_atom)

    def met(self, turn):
        distance = self.distance(turn)
        return lax.rem(self.sign * (1 - 2 * (distance % 2)) * distance + self.n_atom, self.n_atom)

    def block(self, place):
        return lax.rem(self.atom * self.own_b + place + self.blocks - 1, self.blocks)

    def small(self, which):
        source, target = (
            (self.near_hbm, self.near),
            (self.coupling_hbm, self.coupling),
            (self.shifts_hbm, self.shifts),
            (self.occ_hbm, self.occ),
        )[which]
        return pltpu.make_async_copy(source, target, self.small_sem.at[which])

    def load(self, kind, place):
        source, target = ((self.green_hbm, self.green), (self.sigma_hbm, self.sigma))[kind]
        b = self.block(place)
        return pltpu.make_async_copy(source.at[:, b], target.at[:, b], self.in_sem.at[kind, place])

    def start_loads(self, places):
        @pl.loop(*places)
        def _(place):
            self.load(0, place).start()
            self.load(1, place).start()

    def begin(self, partners, send):
        first = self.own_b + 2
        self.start_loads((0, first))
        for which in range(4):
            self.small(which).start()
        barrier = pltpu.get_barrier_semaphore()
        for partner in partners:
            pl.semaphore_signal(barrier, inc=1, device_id=(partner, self.atom), device_id_type=MESH)

        @pl.loop(1, self.n_atom)
        def _(i):
            pl.semaphore_signal(barrier, inc=1, device_id=(self.win, self.owner(i)), device_id_type=MESH)

        early = self.n_atom > 2
        forward = (self.sign + 1) // 2
        if early:
            start = self.own_b * (2 * forward + (self.n_atom - 1) * (1 - forward))
            self.start_loads((start, start + self.own_b))
        for place in range(first):
            self.make_lesser(place)
        self.small(0).wait()
        self.small(1).wait()
        self.make_part(0, self.held)
        pl.semaphore_wait(barrier, len(partners) + self.n_atom - 1)
        send(0)
        if early:
            start = first + self.own_b * forward
            self.start_loads((start, start + self.blocks - first - self.own_b))

    def make_lesser(self, place):
        self.load(0, place).wait()
        self.load(1, place).wait()
        norb, b = self.norb, self.block(place)
        for e in range(self.own_e):
            g = self.green[e, b].reshape(2 * norb, norb)
            s = jnp.concatenate([self.sigma[e, b, 0], self.sigma[e, b, 1]], axis=1)
            product = fold(dot(g, s, (1, 0)), norb)
            self.lesser[e, b] = fold(dot(product, g, (1, 1)), norb).reshape(2, norb, norb)

    def make_part(self, step, target):
        norb, own_e = self.norb, self.own_e
        j = self.owner(step)
        matrices = [self.coupling[d] for d in range(self.coupling.shape[0])]
        for i in range(self.own_b):
            bent = []
            for d, matrix in enumerate(matrices):
                n = self.near[d, j * self.own_b + i]
                tiles = []
                for e in range(own_e):
                    picked = self.lesser[e, n]
                    tiles += [picked[0], picked[1]]
                wide = dot(matrix, jnp.concatenate(tiles, axis=1), (1, 0)).astype(BF16)
                bent.append(
                    jnp.concatenate([wide[:, t * norb : (t + 1) * norb] for t in range(2 * own_e)], axis=0)
                )
            full = dot(jnp.concatenate(bent, axis=1), jnp.concatenate(matrices, axis=1), (1, 1)).astype(BF16)
            for e in range(own_e):
                target[step, e, i] = full[2 * e * norb : 2 * (e + 1) * norb].reshape(2, norb, norb)

    def give(self, step):
        return pltpu.make_async_remote_copy(
            src_ref=self.part.at[step],
            dst_ref=self.held.at[step],
            send_sem=self.give_sem.at[step],
            recv_sem=self.take_sem.at[step],
            device_id=(self.win, self.owner(step)),
            device_id_type=MESH,
        )

    def make_parts(self, send):
        steps = self.n_atom
        lag = min(LAG, steps - 1)

        @pl.loop(1, steps)
        def _(turn):
            offset = self.sent(turn)

            before = self.turn_of((self.distance(turn) + steps - self.sign) % steps)
            after = self.turn_of((self.distance(turn) + steps + self.sign) % steps)

            @pl.when(before > turn)
            def _():
                for i in range(self.own_b):
                    self.make_lesser(self.own_b * offset + i)

            @pl.when(after > turn)
            def _():
                for i in range(self.own_b):
                    self.make_lesser(self.own_b * (offset + 1) + i)

            self.make_part(offset, self.part)
            self.give(offset).start()

            @pl.when(turn == 2)
            def _():
                self.send_held(self.met(1), send)

            @pl.when(turn > lag + 1)
            def _():
                self.send_held(self.met(turn - lag), send)

        @pl.loop(steps - lag, steps)
        def _(turn):
            self.send_held(self.met(turn), send)

    def send_held(self, slot, send):
        self.give(slot).wait_recv()
        send(slot)

    def weights(self):
        self.small(2).wait()
        self.small(3).wait()
        weights = []
        for bit in self.bits:
            weight = jnp.float32(0.0)
            for mode in range(self.shifts.shape[0]):
                weight = weight + jnp.where(self.shifts[mode] == bit, self.occ[mode], 0.0)
            weights.append(weight)
        return weights

    def store(self, slot, e, i, value):
        sender = lax.rem(self.atom + self.n_atom - slot, self.n_atom)
        self.out[sender * self.own_e + e, i] = value.astype(BF16)

    def given(self, slot):
        @pl.when(slot > 0)
        def _():
            self.give(slot).wait_send()


def near_kernel(bits, n_atom, *refs):
    here = Context(bits, n_atom, refs[:20])
    got, send_sem, recv_sem = refs[20:]
    partners = [flip(here.win, bit) for bit in bits]
    count = len(bits)

    def pass_to(k, slot):
        return pltpu.make_async_remote_copy(
            src_ref=here.held.at[slot],
            dst_ref=got.at[k, slot],
            send_sem=send_sem.at[k, slot],
            recv_sem=recv_sem.at[k, slot],
            device_id=(partners[k], here.atom),
            device_id_type=MESH,
        )

    def send(slot):
        for k in range(count):
            pass_to(k, slot).start()

    here.begin(partners, send)
    here.make_parts(send)
    weights = here.weights()

    @pl.loop(0, n_atom)
    def _(turn):
        slot = here.met(turn)
        here.given(slot)
        for k in range(count):
            pass_to(k, slot).wait()
        for e in range(here.own_e):
            for i in range(here.own_b):
                summed = weights[0] * got[0, slot, e, i].astype(F32)
                for k in range(1, count):
                    summed = summed + weights[k] * got[k, slot, e, i].astype(F32)
                here.store(slot, e, i, summed)


def far_kernel(bits, n_atom, *refs):
    here = Context(bits, n_atom, refs[:20])
    got_first, got_away, got_on, got_sum, got_top, mixed, half_send, half_recv, top_send, top_recv = refs[20:]
    half = here.own_e // 2
    lead, rest = pl.ds(0, half), pl.ds(half, half)
    twin = flip(here.win, bits[0])
    cross = flip(twin, bits[1])
    across = flip(here.win, bits[2])

    def hop(kind, slot):
        source, target, win = (
            (here.held.at[slot, lead], got_first.at[slot], twin),
            (here.held.at[slot, rest], got_away.at[slot], cross),
            (got_first.at[slot], got_on.at[slot], cross),
            (mixed.at[slot], got_sum.at[slot], twin),
        )[kind]
        return pltpu.make_async_remote_copy(
            src_ref=source,
            dst_ref=target,
            send_sem=half_send.at[kind, slot],
            recv_sem=half_recv.at[kind, slot],
            device_id=(win, here.atom),
            device_id_type=MESH,
        )

    def top(slot):
        return pltpu.make_async_remote_copy(
            src_ref=here.held.at[slot],
            dst_ref=got_top.at[slot],
            send_sem=top_send.at[slot],
            recv_sem=top_recv.at[slot],
            device_id=(across, here.atom),
            device_id_type=MESH,
        )

    def send(slot):
        hop(0, slot).start()
        hop(1, slot).start()

    here.begin([twin, cross, across], send)
    here.make_parts(send)
    low, mid, high = here.weights()

    def pass_on(slot):
        hop(0, slot).wait_recv()
        hop(2, slot).start()
        top(slot).start()
        hop(1, slot).wait_recv()
        for e in range(half):
            for i in range(here.own_b):
                summed = low * here.held[slot, half + e, i].astype(F32) + mid * got_away[slot, e, i].astype(F32)
                mixed[slot, e, i] = summed.astype(BF16)
        hop(3, slot).start()

    @pl.loop(0, n_atom)
    def _(turn):
        pass_on(here.met(turn))

    @pl.loop(0, n_atom)
    def _(turn):
        slot = here.met(turn)
        here.given(slot)
        hop(0, slot).wait_send()
        hop(1, slot).wait_send()
        hop(2, slot).wait()
        hop(3, slot).wait()
        top(slot).wait()
        for e in range(half):
            for i in range(here.own_b):
                summed = low * got_first[slot, e, i].astype(F32) + mid * got_on[slot, e, i].astype(F32)
                here.store(slot, e, i, summed + high * got_top[slot, e, i].astype(F32))
                summed = got_sum[slot, e, i].astype(F32) + high * got_top[slot, half + e, i].astype(F32)
                here.store(slot, half + e, i, summed)


def call(bits, n_atom, retarded, sigma_in, bit_shifts, occupation, neighbors, coupling):
    own_e, blocks, _, norb, _ = retarded.shape
    own_b = blocks // n_atom
    pieces = (n_atom, own_e, own_b, 2, norb, norb)
    halves = (n_atom, own_e // 2, own_b, 2, norb, norb)
    count = len(bits)
    dma = pltpu.SemaphoreType.DMA
    if bits[1] == 1:
        body = near_kernel
        extra = [pltpu.VMEM((count, *pieces), BF16), dma((count, n_atom)), dma((count, n_atom))]
    else:
        body = far_kernel
        extra = [pltpu.VMEM(halves, BF16) for _ in range(4)]
        extra += [pltpu.VMEM(pieces, BF16), pltpu.VMEM(halves, BF16)]
        extra += [dma((4, n_atom)), dma((4, n_atom)), dma((n_atom,)), dma((n_atom,))]
    return pl.pallas_call(
        functools.partial(body, bits, n_atom),
        out_shape=jax.ShapeDtypeStruct((own_e * n_atom, own_b, 2, norb, norb), BF16),
        in_specs=[pl.BlockSpec(memory_space=pl.ANY)] * 6,
        out_specs=pl.BlockSpec(memory_space=pltpu.VMEM),
        scratch_shapes=[
            pltpu.SMEM(bit_shifts.shape, jnp.int32),
            pltpu.SMEM(occupation.shape, F32),
            pltpu.SMEM(neighbors.shape[::-1], jnp.int32),
            pltpu.VMEM(coupling.shape, BF16),
            pltpu.VMEM(retarded.shape, BF16),
            pltpu.VMEM(retarded.shape, BF16),
            pltpu.VMEM(retarded.shape, BF16),
            pltpu.VMEM(pieces, BF16),
            pltpu.VMEM(pieces, BF16),
            dma((4,)),
            dma((2, blocks)),
            dma((n_atom,)),
            dma((n_atom,)),
            *extra,
        ],
        compiler_params=pltpu.CompilerParams(
            collective_id=bits[1], has_side_effects=True, vmem_limit_bytes=50 * 2**20
        ),
        name="self_energy",
    )(bit_shifts, occupation, neighbors.T, retarded, sigma_in, coupling)


def on_device(retarded, sigma_in, bit_shifts, occupation, neighbors, coupling):
    n_atom = lax.axis_size("atom")
    top = lax.axis_size("win").bit_length() - 2
    return lax.cond(
        jnp.any(bit_shifts == 1),
        functools.partial(call, (0, 1, top), n_atom),
        functools.partial(call, (0, 2, top), n_atom),
        retarded,
        sigma_in,
        bit_shifts,
        occupation,
        neighbors,
        coupling,
    )


def solution(mesh):
    return jax.shard_map(
        on_device,
        mesh=mesh,
        in_specs=(
            P(("win", "atom"), None, None, None, None),
            P(("win", "atom"), None, None, None, None),
            P(),
            P(),
            P(),
            P(),
        ),
        out_specs=P("win", "atom", None, None, None),
        check_vma=False,
    )
```

```python
import functools

import jax
import jax.numpy as jnp
from jax import lax
from jax.experimental import pallas as pl
from jax.experimental.pallas import tpu as pltpu
from jax.sharding import PartitionSpec as P

MESH = pl.DeviceIdType.MESH
F32 = jnp.float32
BF16 = jnp.bfloat16
LAG = 2
STRIDE = 11


def dot(left, right, contract):
    return lax.dot_general(left, right, ((contract[0:1], contract[1:2]), ((), ())), preferred_element_type=F32)


def fold(quad, norb):
    real = quad[:norb, :norb] - quad[norb:, norb:]
    imag = quad[:norb, norb:] + quad[norb:, :norb]
    return jnp.concatenate([real, imag], axis=0).astype(BF16)


def flip(win, bit):
    mask = 2**bit
    return win + mask * (1 - 2 * ((win // mask) % 2))


class Context:
    def __init__(self, bits, n_atom, refs):
        (
            self.shifts_hbm,
            self.occ_hbm,
            self.near_hbm,
            self.green_hbm,
            self.sigma_hbm,
            self.coupling_hbm,
            self.out,
            self.shifts,
            self.occ,
            self.near,
            self.coupling,
            self.green,
            self.sigma,
            self.lesser,
            self.part,
            self.held,
            self.small_sem,
            self.in_sem,
            self.give_sem,
            self.take_sem,
        ) = refs
        self.bits = bits
        self.n_atom = n_atom
        self.own_e = self.green.shape[0]
        self.blocks = self.lesser.shape[1]
        self.own_b = self.blocks // n_atom
        self.norb = self.green.shape[-1]
        self.win = lax.axis_index("win")
        self.atom = lax.axis_index("atom")
        self.sign = 1 - 2 * (self.atom % 2)

    def owner(self, offset):
        return lax.rem(self.atom + offset, self.n_atom)

    def swapped(self, value):
        other = STRIDE % self.n_atom
        return jnp.where(value == 1, other, jnp.where(value == other, 1, value))

    def distance(self, turn):
        return self.swapped((STRIDE * turn) % self.n_atom)

    def turn_of(self, distance):
        return (pow(STRIDE, -1, self.n_atom) * self.swapped(distance)) % self.n_atom

    def sent(self, turn):
        return lax.rem(self.sign * self.distance(turn) + self.n_atom, self.n_atom)

    def met(self, turn):
        distance = self.distance(turn)
        return lax.rem(self.sign * (1 - 2 * (distance % 2)) * distance + self.n_atom, self.n_atom)

    def block(self, place):
        return lax.rem(self.atom * self.own_b + place + self.blocks - 1, self.blocks)

    def small(self, which):
        source, target = (
            (self.near_hbm, self.near),
            (self.coupling_hbm, self.coupling),
            (self.shifts_hbm, self.shifts),
            (self.occ_hbm, self.occ),
        )[which]
        return pltpu.make_async_copy(source, target, self.small_sem.at[which])

    def load(self, kind, place):
        source, target = ((self.green_hbm, self.green), (self.sigma_hbm, self.sigma))[kind]
        b = self.block(place)
        return pltpu.make_async_copy(source.at[:, b], target.at[:, b], self.in_sem.at[kind, place])

    def start_loads(self, places):
        @pl.loop(*places)
        def _(place):
            self.load(0, place).start()
            self.load(1, place).start()

    def begin(self, partners, send):
        first = self.own_b + 2
        self.start_loads((0, first))
        for which in range(4):
            self.small(which).start()
        barrier = pltpu.get_barrier_semaphore()
        for partner in partners:
            pl.semaphore_signal(barrier, inc=1, device_id=(partner, self.atom), device_id_type=MESH)

        @pl.loop(1, self.n_atom)
        def _(i):
            pl.semaphore_signal(barrier, inc=1, device_id=(self.win, self.owner(i)), device_id_type=MESH)

        early = self.n_atom > 2
        forward = (self.sign + 1) // 2
        if early:
            start = self.own_b * (2 * forward + (self.n_atom - 1) * (1 - forward))
            self.start_loads((start, start + self.own_b))
        for place in range(first):
            self.make_lesser(place)
        self.small(0).wait()
        self.small(1).wait()
        self.make_part(0, self.held)
        pl.semaphore_wait(barrier, len(partners) + self.n_atom - 1)
        send(0)
        if early:
            start = first + self.own_b * forward
            self.start_loads((start, start + self.blocks - first - self.own_b))

    def make_lesser(self, place):
        self.load(0, place).wait()
        self.load(1, place).wait()
        norb, b = self.norb, self.block(place)
        for e in range(self.own_e):
            g = self.green[e, b].reshape(2 * norb, norb)
            s = jnp.concatenate([self.sigma[e, b, 0], self.sigma[e, b, 1]], axis=1)
            product = fold(dot(g, s, (1, 0)), norb)
            self.lesser[e, b] = fold(dot(product, g, (1, 1)), norb).reshape(2, norb, norb)

    def make_part(self, step, target):
        norb, own_e = self.norb, self.own_e
        j = self.owner(step)
        matrices = [self.coupling[d] for d in range(self.coupling.shape[0])]
        for i in range(self.own_b):
            bent = []
            for d, matrix in enumerate(matrices):
                n = self.near[d, j * self.own_b + i]
                tiles = []
                for e in range(own_e):
                    picked = self.lesser[e, n]
                    tiles += [picked[0], picked[1]]
                wide = dot(matrix, jnp.concatenate(tiles, axis=1), (1, 0)).astype(BF16)
                bent.append(
                    jnp.concatenate([wide[:, t * norb : (t + 1) * norb] for t in range(2 * own_e)], axis=0)
                )
            full = dot(jnp.concatenate(bent, axis=1), jnp.concatenate(matrices, axis=1), (1, 1)).astype(BF16)
            for e in range(own_e):
                target[step, e, i] = full[2 * e * norb : 2 * (e + 1) * norb].reshape(2, norb, norb)

    def give(self, step):
        return pltpu.make_async_remote_copy(
            src_ref=self.part.at[step],
            dst_ref=self.held.at[step],
            send_sem=self.give_sem.at[step],
            recv_sem=self.take_sem.at[step],
            device_id=(self.win, self.owner(step)),
            device_id_type=MESH,
        )

    def make_parts(self, send):
        steps = self.n_atom
        lag = min(LAG, steps - 1)

        @pl.loop(1, steps)
        def _(turn):
            offset = self.sent(turn)

            before = self.turn_of((self.distance(turn) + steps - self.sign) % steps)
            after = self.turn_of((self.distance(turn) + steps + self.sign) % steps)

            @pl.when(before > turn)
            def _():
                for i in range(self.own_b):
                    self.make_lesser(self.own_b * offset + i)

            @pl.when(after > turn)
            def _():
                for i in range(self.own_b):
                    self.make_lesser(self.own_b * (offset + 1) + i)

            self.make_part(offset, self.part)
            self.give(offset).start()

            @pl.when(turn == 2)
            def _():
                self.send_held(self.met(1), send)

            @pl.when(turn > lag + 1)
            def _():
                self.send_held(self.met(turn - lag), send)

        @pl.loop(steps - lag, steps)
        def _(turn):
            self.send_held(self.met(turn), send)

    def send_held(self, slot, send):
        self.give(slot).wait_recv()
        send(slot)

    def weights(self):
        self.small(2).wait()
        self.small(3).wait()
        weights = []
        for bit in self.bits:
            weight = jnp.float32(0.0)
            for mode in range(self.shifts.shape[0]):
                weight = weight + jnp.where(self.shifts[mode] == bit, self.occ[mode], 0.0)
            weights.append(weight)
        return weights

    def store(self, slot, e, i, value):
        sender = lax.rem(self.atom + self.n_atom - slot, self.n_atom)
        self.out[sender * self.own_e + e, i] = value.astype(BF16)

    def given(self, slot):
        @pl.when(slot > 0)
        def _():
            self.give(slot).wait_send()


def near_kernel(bits, n_atom, *refs):
    here = Context(bits, n_atom, refs[:20])
    got, send_sem, recv_sem = refs[20:]
    partners = [flip(here.win, bit) for bit in bits]
    count = len(bits)

    def pass_to(k, slot):
        return pltpu.make_async_remote_copy(
            src_ref=here.held.at[slot],
            dst_ref=got.at[k, slot],
            send_sem=send_sem.at[k, slot],
            recv_sem=recv_sem.at[k, slot],
            device_id=(partners[k], here.atom),
            device_id_type=MESH,
        )

    def send(slot):
        for k in range(count):
            pass_to(k, slot).start()

    here.begin(partners, send)
    here.make_parts(send)
    weights = here.weights()

    @pl.loop(0, n_atom)
    def _(turn):
        slot = here.met(turn)
        here.given(slot)
        for k in range(count):
            pass_to(k, slot).wait()
        for e in range(here.own_e):
            for i in range(here.own_b):
                summed = weights[0] * got[0, slot, e, i].astype(F32)
                for k in range(1, count):
                    summed = summed + weights[k] * got[k, slot, e, i].astype(F32)
                here.store(slot, e, i, summed)


def far_kernel(bits, n_atom, *refs):
    here = Context(bits, n_atom, refs[:20])
    got_first, got_away, got_on, got_sum, got_top, mixed, half_send, half_recv, top_send, top_recv = refs[20:]
    half = here.own_e // 2
    lead, rest = pl.ds(0, half), pl.ds(half, half)
    twin = flip(here.win, bits[0])
    cross = flip(twin, bits[1])
    across = flip(here.win, bits[2])

    def hop(kind, slot):
        source, target, win = (
            (here.held.at[slot, lead], got_first.at[slot], twin),
            (here.held.at[slot, rest], got_away.at[slot], cross),
            (got_first.at[slot], got_on.at[slot], cross),
            (mixed.at[slot], got_sum.at[slot], twin),
        )[kind]
        return pltpu.make_async_remote_copy(
            src_ref=source,
            dst_ref=target,
            send_sem=half_send.at[kind, slot],
            recv_sem=half_recv.at[kind, slot],
            device_id=(win, here.atom),
            device_id_type=MESH,
        )

    def top(slot):
        return pltpu.make_async_remote_copy(
            src_ref=here.held.at[slot],
            dst_ref=got_top.at[slot],
            send_sem=top_send.at[slot],
            recv_sem=top_recv.at[slot],
            device_id=(across, here.atom),
            device_id_type=MESH,
        )

    def send(slot):
        hop(0, slot).start()
        hop(1, slot).start()

    here.begin([twin, cross, across], send)
    here.make_parts(send)
    low, mid, high = here.weights()

    def pass_on(slot):
        hop(0, slot).wait_recv()
        hop(2, slot).start()
        top(slot).start()
        hop(1, slot).wait_recv()
        for e in range(half):
            for i in range(here.own_b):
                summed = low * here.held[slot, half + e, i].astype(F32) + mid * got_away[slot, e, i].astype(F32)
                mixed[slot, e, i] = summed.astype(BF16)
        hop(3, slot).start()

    @pl.loop(0, n_atom)
    def _(turn):
        pass_on(here.met(turn))

    @pl.loop(0, n_atom)
    def _(turn):
        slot = here.met(turn)
        here.given(slot)
        hop(0, slot).wait_send()
        hop(1, slot).wait_send()
        hop(2, slot).wait()
        hop(3, slot).wait()
        top(slot).wait()
        for e in range(half):
            for i in range(here.own_b):
                summed = low * got_first[slot, e, i].astype(F32) + mid * got_on[slot, e, i].astype(F32)
                here.store(slot, e, i, summed + high * got_top[slot, e, i].astype(F32))
                summed = got_sum[slot, e, i].astype(F32) + high * got_top[slot, half + e, i].astype(F32)
                here.store(slot, half + e, i, summed)


def call(bits, n_atom, retarded, sigma_in, bit_shifts, occupation, neighbors, coupling):
    own_e, blocks, _, norb, _ = retarded.shape
    own_b = blocks // n_atom
    pieces = (n_atom, own_e, own_b, 2, norb, norb)
    halves = (n_atom, own_e // 2, own_b, 2, norb, norb)
    count = len(bits)
    dma = pltpu.SemaphoreType.DMA
    if bits[1] == 1:
        body = near_kernel
        extra = [pltpu.VMEM((count, *pieces), BF16), dma((count, n_atom)), dma((count, n_atom))]
    else:
        body = far_kernel
        extra = [pltpu.VMEM(halves, BF16) for _ in range(4)]
        extra += [pltpu.VMEM(pieces, BF16), pltpu.VMEM(halves, BF16)]
        extra += [dma((4, n_atom)), dma((4, n_atom)), dma((n_atom,)), dma((n_atom,))]
    return pl.pallas_call(
        functools.partial(body, bits, n_atom),
        out_shape=jax.ShapeDtypeStruct((own_e * n_atom, own_b, 2, norb, norb), BF16),
        in_specs=[pl.BlockSpec(memory_space=pl.ANY)] * 6,
        out_specs=pl.BlockSpec(memory_space=pltpu.VMEM),
        scratch_shapes=[
            pltpu.SMEM(bit_shifts.shape, jnp.int32),
            pltpu.SMEM(occupation.shape, F32),
            pltpu.SMEM(neighbors.shape[::-1], jnp.int32),
            pltpu.VMEM(coupling.shape, BF16),
            pltpu.VMEM(retarded.shape, BF16),
            pltpu.VMEM(retarded.shape, BF16),
            pltpu.VMEM(retarded.shape, BF16),
            pltpu.VMEM(pieces, BF16),
            pltpu.VMEM(pieces, BF16),
            dma((4,)),
            dma((2, blocks)),
            dma((n_atom,)),
            dma((n_atom,)),
            *extra,
        ],
        compiler_params=pltpu.CompilerParams(
            collective_id=bits[1], has_side_effects=True, vmem_limit_bytes=50 * 2**20
        ),
        name="self_energy",
    )(bit_shifts, occupation, neighbors.T, retarded, sigma_in, coupling)


def on_device(retarded, sigma_in, bit_shifts, occupation, neighbors, coupling):
    n_atom = lax.axis_size("atom")
    top = lax.axis_size("win").bit_length() - 2
    return lax.cond(
        jnp.any(bit_shifts == 1),
        functools.partial(call, (0, 1, top), n_atom),
        functools.partial(call, (0, 2, top), n_atom),
        retarded,
        sigma_in,
        bit_shifts,
        occupation,
        neighbors,
        coupling,
    )


def solution(mesh):
    return jax.shard_map(
        on_device,
        mesh=mesh,
        in_specs=(
            P(("win", "atom"), None, None, None, None),
            P(("win", "atom"), None, None, None, None),
            P(),
            P(),
            P(),
            P(),
        ),
        out_specs=P("win", "atom", None, None, None),
        check_vma=False,
    )
```
